32 devices in a mesh: slab: 16 (over z, x, core), mem: 2 (over y).
Axes of the slice: x: 2, y: 2, z: 4, core: 2. Of those that a mesh axis runs over, the one named last changes fastest.
Arguments:
- anomalies: bfloat16 [16, 12, 512, 128], P('mem', None, 'slab'), may hold values from -6 to 6
- grad_in: float32 [12, 512, 128], P(None, 'slab'), may hold values from -6 to 6
- alpha: float32 [16, 12, 512, 128], P('mem', None, 'slab'), may hold values from -0.18 to 0.18
- land_sea: int32 [12, 512, 128], P(None, 'slab'), may hold values 0 or 1
- length_rates: float32 [2, 512, 128], P(None, 'slab'), may hold values from 0.125 to 0.25
- step_counts: int32 [2, 12], replicated, may hold values from 6 to 8, as said below
Outputs:
- direction: float32 [16, 12, 512, 128], P('mem', None, 'slab')
- grad_norm: float32 [], replicated
The draws below stay inside these ranges and needn't reach their ends.
Inputs may be any that keep to these rules, and one draw needn't show every extreme that they name: `step_counts`: each level's number of transposed diffusion steps in each pass; in every draw some level takes 8 steps in both passes, and 6 is reached.
All inputs are finite; a program needn't handle non-finite values. No bound on the sum of `land_sea` on one device may be relied on, other than what follows from the above.
Results may differ from the reference program's by a relative error of at most 0.0003.
Values sent between devices are 32-bit elements; how exact they have to be, the bound alone decides.
A program may use at most 64 MiB of HBM per device.

```python
import jax
import jax.numpy as jnp
from jax import lax

LV = 12
NY = 128
NSTEP = 8
MEMBERS = 16
NX = 512


def draw_step_counts(key, part):
    key = jax.random.fold_in(key, 11)
    first, second, third, fourth = jax.random.split(key, 4)
    counts = jax.random.randint(first, (2, LV), NSTEP - 2, NSTEP + 1)
    full_level = jax.random.randint(second, (), 0, LV)
    low_level = (full_level + 1 + jax.random.randint(third, (), 0, LV - 1)) % LV
    low_pass = jax.random.randint(fourth, (), 0, 2)
    levels = jnp.arange(LV)[None, :]
    passes = jnp.arange(2)[:, None]
    counts = jnp.where(levels == full_level, NSTEP, counts)
    counts = jnp.where((levels == low_level) & (passes == low_pass), NSTEP - 2, counts)
    return counts.astype(jnp.int32)


def with_ends(result, stream_key, low, high):
    shape = result.shape
    index_at = [jax.random.randint(jax.random.fold_in(stream_key, axis), (), 0, shape[axis]) for axis in range(len(shape))]
    result = result.at[tuple(index_at)].set(low)
    longest = shape.index(max(shape))
    index_at[longest] = (index_at[longest] + 1) % shape[longest]
    return result.at[tuple(index_at)].set(high)


def steps_of(stream_key, extent, cuts, least, largest):
    gain = 1.0
    for dim, parts in cuts:
        draws = jax.random.uniform(jax.random.fold_in(jax.random.fold_in(stream_key, 6), dim), (parts,), jnp.float32, least / len(cuts), largest / len(cuts))
        gain = gain * jnp.repeat(jnp.exp(draws), extent[dim] // parts).reshape((-1,) + (1,) * (len(extent) - 1 - dim))
    return gain


def gaussian(own_key, shape, scale, limit, pieces=(), kind=jnp.bfloat16):
    array = jax.random.normal(own_key, shape, jnp.float32) * scale
    if len(pieces) > 0:
        array = steps_of(own_key, shape, pieces, -0.22, 0.18) * array
    return jnp.clip(array, min=-limit, max=limit).astype(kind)


def setup_inputs(seed: int = 0) -> dict:
    splits = jax.random.split(jax.random.key(seed), 7)
    anomalies = gaussian(splits[0], (MEMBERS, LV, NX, NY), 1.0, 6.0, ((0, 2), (2, 16)))
    grad_in = gaussian(splits[1], (LV, NX, NY), 1.0, 6.0, ((1, 16),), jnp.float32)
    alpha = gaussian(splits[2], (MEMBERS, LV, NX, NY), 0.03, 0.18, ((0, 2), (2, 16)), jnp.float32)
    land_sea = with_ends((jax.random.randint(splits[3], (LV, NX, NY), 0, 8) < 7).astype(jnp.int32), jax.random.fold_in(splits[3], 1), 0, 1)
    length_rates = jnp.clip(0.125 + 0.125 * jax.random.uniform(splits[4], (2, NX, NY), jnp.float32) ** steps_of(splits[4], (2, NX, NY), ((1, 16),), -0.2, 0.2), 0.125, 0.25)
    step_counts = draw_step_counts(jax.random.fold_in(splits[6], 71), 0)
    return dict(anomalies=anomalies, grad_in=grad_in, alpha=alpha, land_sea=land_sea, length_rates=length_rates, step_counts=step_counts)


def transposed_step(padded, ocean, rates, active):
    weighted = rates * padded
    face_x = ocean[:, 1:, :] * ocean[:, :-1, :]
    flux_x = face_x * (weighted[:, :, 1:, :] - weighted[:, :, :-1, :])
    lap_x = flux_x[:, :, 1:, :] - flux_x[:, :, :-1, :]
    inner = weighted[:, :, 1:-1, :]
    ocean_in = ocean[:, 1:-1, :]
    face_y = ocean_in[:, :, 1:] * ocean_in[:, :, :-1]
    flux_y = face_y * (inner[..., 1:] - inner[..., :-1])
    flux_y = jnp.pad(flux_y, ((0, 0), (0, 0), (0, 0), (1, 1)))
    lap_y = flux_y[..., 1:] - flux_y[..., :-1]
    return padded[:, :, 1:-1, :] + active[:, None, None] * (lap_x + lap_y)

def wrap_pad(values, axis):
    size = values.shape[axis]
    first = lax.slice_in_dim(values, 0, 1, axis=axis)
    last = lax.slice_in_dim(values, size - 1, size, axis=axis)
    return jnp.concatenate([last, values, first], axis=axis)

def reference(anomalies, grad_in, alpha, land_sea, length_rates, step_counts):
    ocean = land_sea.astype(jnp.float32)
    ocean_pad = wrap_pad(ocean, 1)
    rates_pad = [wrap_pad(length_rates[p], 0) for p in range(2)]

    def one_member(pair):
        anomaly, control = pair
        field = (anomaly.astype(jnp.float32) * grad_in)[None]
        for p in (1, 0):
            for s in range(NSTEP):
                active = (s < step_counts[p]).astype(jnp.float32)
                field = transposed_step(wrap_pad(field, 2), ocean_pad, rates_pad[p], active)
        return control + field[0]
    grad = lax.map(one_member, (anomalies, alpha))
    mean = lax.optimization_barrier(jnp.sum(grad, axis=0)) / MEMBERS
    projected = grad - mean
    total = jnp.sum(projected * projected)
    scale = jnp.sqrt(total / (MEMBERS * LV * NX * NY) + 1e-06)
    return (projected / scale, jnp.sqrt(total))
```

```python
import functools

import jax
import jax.numpy as jnp
from jax import lax
from jax.experimental import pallas as pl
from jax.experimental.pallas import tpu as pltpu
from jax.sharding import PartitionSpec as P

NSTEP = 8
SURE = 6
W = NSTEP
SKEW = 2
MESH = pl.DeviceIdType.MESH


def kernel(
    ns, nm, count_all, members_all,
    cnt, anom, gin, land, rate, alpha_any, proj_any, stats,
    u0, u1, u2, hal, ohal, rhal, oc, coef, alpha, g, msum, mrecv, tsend, trecv,
    hsend, hrecv, csend, crecv, msend, mrecv_sem, tsend_sem, trecv_sem, loc_sem,
    out_sem,
):
    nmem, levels, nx, ny = anom.shape
    nall = ns * nm
    s = lax.axis_index("slab")
    q = lax.axis_index("mem")
    me = s * nm + q
    left = (lax.rem(s + ns - 1, ns), q)
    right = (lax.rem(s + 1, ns), q)

    def other(d):
        i = lax.rem(me + d, nall)
        return (lax.div(i, nm), lax.rem(i, nm))

    barrier = pltpu.get_barrier_semaphore()

    @pl.loop(1, nall)
    def _(d):
        pl.semaphore_signal(barrier, inc=1, device_id=other(d), device_id_type=MESH)

    acopy = pltpu.make_async_copy(alpha_any, alpha, loc_sem)
    acopy.start()
    pl.semaphore_wait(barrier, nall - 1)

    def rdma(src, dst, ss, rs, dev):
        return pltpu.make_async_remote_copy(
            src_ref=src, dst_ref=dst, send_sem=ss, recv_sem=rs, device_id=dev,
            device_id_type=MESH,
        )

    def coef_copies():
        res = []
        for side, lo, dev in ((1, 0, left), (0, nx - W, right)):
            res.append(rdma(land.at[:, pl.ds(lo, W), :], ohal.at[side],
                            csend.at[0, side], crecv.at[0, side], dev))
            res.append(rdma(rate.at[:, pl.ds(lo, W), :], rhal.at[side],
                            csend.at[1, side], crecv.at[1, side], dev))
        return res

    def halo_copies(u, p, l):
        rows = W * nmem
        return [
            rdma(u.at[l, pl.ds(lo, rows), :], hal.at[p, side, l],
                 hsend.at[p, side, l], hrecv.at[p, side, l], dev)
            for side, lo, dev in ((1, 0, left), (0, nx * nmem - rows, right))
        ]

    def mean_copies(l):
        return [
            rdma(msum.at[l], mrecv.at[k - 1, l], msend.at[k - 1, l],
                 mrecv_sem.at[k - 1, l], (s, lax.rem(q + k, nm)))
            for k in range(1, nm)
        ]

    def out_copy(l):
        return pltpu.make_async_copy(g.at[:, l], proj_any.at[:, l], out_sem.at[l])

    for c in coef_copies():
        c.start()

    @pl.loop(0, levels)
    def _(l):
        for h in range(nx // 16):
            facs = []
            for t in (2 * h, 2 * h + 1):
                sl = pl.ds(8 * t, 8)
                facs.append(gin[l, sl, :] * (rate[1, sl, :] * land[l, sl, :].astype(jnp.float32)))
            for m in range(nmem):
                a = anom[m, l, pl.ds(16 * h, 16), :].astype(jnp.float32)
                for j in range(2):
                    u0[l, pl.ds((16 * h + 8 * j) * nmem + m, 8, stride=nmem), :] = (
                        a[8 * j:8 * j + 8] * facs[j]
                    )
        for c in halo_copies(u0, 0, l):
            c.start()

    for c in coef_copies():
        c.wait()

    lane = lax.broadcasted_iota(jnp.int32, (8, ny), 1)
    not_first = lane > 0
    not_last = lane < ny - 1

    def sides(v):
        return (jnp.where(not_first, pltpu.roll(v, 1, 1), 0.0)
                + jnp.where(not_last, pltpu.roll(v, ny - 1, 1), 0.0))

    ext = nx + 2 * W
    zero = jnp.zeros((8, ny), jnp.float32)
    oc[pl.ds(0, 8), :] = zero
    oc[pl.ds(8 + ext, 8), :] = zero

    def rates_at(p, t):
        if t == 0:
            return rhal[0, p]
        if t == ext // 8 - 1:
            return rhal[1, p]
        return rate[p, pl.ds(8 * t - W, 8), :]

    def make_coefs(l):
        oc[pl.ds(8, 8), :] = ohal[0, l].astype(jnp.float32)
        for t in range(nx // 8):
            oc[pl.ds(8 + W + 8 * t, 8), :] = land[l, pl.ds(8 * t, 8), :].astype(jnp.float32)
        oc[pl.ds(8 + W + nx, 8), :] = ohal[1, l].astype(jnp.float32)
        for t in range(ext // 8):
            o = oc[pl.ds(8 + 8 * t, 8), :]
            around = oc[pl.ds(7 + 8 * t, 8), :] + oc[pl.ds(9 + 8 * t, 8), :] + sides(o)
            for p in (1, 0):
                k = o * rates_at(p, t)
                coef[p, 0, l, pl.ds(8 * t, 8), :] = k
                coef[p, 1, l, pl.ds(8 * t, 8), :] = 1.0 - k * around

    def wide(row):
        return jnp.broadcast_to(row, (nmem, ny))

    def run(order, p, l, src, put):
        steps = jnp.full((nmem, ny), cnt[p, l], jnp.int32)
        masks = {t: steps >= t for t in range(SURE + 1, NSTEP + 1)}
        vals = [{} for _ in range(NSTEP + 1)]
        for d in range(-W, nx + W + SKEW * NSTEP + 1):
            if d < nx + W:
                if d < 0:
                    v = hal[order, 0, l, pl.ds((d + W) * nmem, nmem), :]
                elif d < nx:
                    v = src[l, pl.ds(d * nmem, nmem), :]
                else:
                    v = hal[order, 1, l, pl.ds((d - nx) * nmem, nmem), :]
                vals[0][d] = v
            for t in range(1, NSTEP + 1):
                x = d - SKEW * t
                if not -(W - t) <= x <= nx - 1 + W - t:
                    continue
                old = vals[t - 1]
                v = old[x]
                k = wide(coef[p, 0, l, pl.ds(x + W, 1), :])
                a = wide(coef[p, 1, l, pl.ds(x + W, 1), :])
                new = a * v + k * ((old[x - 1] + old[x + 1]) + sides(v))
                if t > SURE:
                    new = jnp.where(masks[t], new, v)
                if t == NSTEP:
                    put(x, new)
                else:
                    vals[t][x] = new

    @pl.loop(0, levels)
    def _(l):
        make_coefs(l)
        for c in halo_copies(u0, 0, l):
            c.wait_recv()

        def put(x, v):
            ratio = rate[0, pl.ds(x, 1), :] / rate[1, pl.ds(x, 1), :]
            u1[l, pl.ds(x * nmem, nmem), :] = v * wide(ratio)

        run(0, 1, l, u0, put)
        for c in halo_copies(u1, 1, l):
            c.start()

    acopy.wait()

    @pl.loop(0, levels)
    def _(l):
        for c in halo_copies(u1, 1, l):
            c.wait_recv()

        def put(x, v):
            u2[pl.ds(x * nmem, nmem), :] = v

        run(1, 0, l, u1, put)
        for h in range(nx // 16):
            cs = []
            for t in (2 * h, 2 * h + 1):
                sl = pl.ds(8 * t, 8)
                cs.append((gin[l, sl, :], land[l, sl, :] > 0, 1.0 / rate[0, sl, :]))
            tot = [zero, zero]
            for m in range(nmem):
                a = anom[m, l, pl.ds(16 * h, 16), :].astype(jnp.float32)
                for j in range(2):
                    gi, wet, inv = cs[j]
                    x = 16 * h + 8 * j
                    u = u2[pl.ds(x * nmem + m, 8, stride=nmem), :]
                    v = alpha[m, l, pl.ds(x, 8), :] + jnp.where(wet, u * inv, a[8 * j:8 * j + 8] * gi)
                    g[m, l, pl.ds(x, 8), :] = v
                    tot[j] = tot[j] + v
            for j in range(2):
                msum[l, pl.ds(16 * h + 8 * j, 8), :] = tot[j]
        for c in mean_copies(l):
            c.start()

    def project(l, acc):
        for c in mean_copies(l):
            c.wait_recv()
        acc = list(acc)
        for t in range(nx // 8):
            sl = pl.ds(8 * t, 8)
            mean = msum[l, sl, :]
            for k in range(nm - 1):
                mean = mean + mrecv[k, l, sl, :]
            mean = mean * (1.0 / members_all)
            for m in range(nmem):
                v = g[m, l, sl, :] - mean
                g[m, l, sl, :] = v
                acc[m % 4] = acc[m % 4] + v * v
        out_copy(l).start()
        return tuple(acc)

    acc = lax.fori_loop(0, levels, project, (zero,) * 4)
    own = (acc[0] + acc[1]) + (acc[2] + acc[3])
    tsend[...] = own

    def total_copy(d):
        return rdma(tsend, trecv.at[d], tsend_sem.at[d], trecv_sem.at[d], other(d))

    @pl.loop(1, nall)
    def _(d):
        total_copy(d).start()

    @pl.loop(0, levels)
    def _(l):
        for p, u in ((0, u0), (1, u1)):
            for c in halo_copies(u, p, l):
                c.wait_send()
        for c in mean_copies(l):
            c.wait_send()
        out_copy(l).wait()

    trecv[0] = own

    @pl.loop(1, nall)
    def _(d):
        total_copy(d).wait()

    def add(i, a):
        return a + trecv[lax.rem(me - i + nall, nall)]

    whole = lax.fori_loop(0, nall, add, zero)
    total = jnp.full((8, ny), jnp.sum(whole), jnp.float32)
    stats[0] = jnp.sqrt(total)
    stats[1] = 1.0 / jnp.sqrt(total * (1.0 / count_all) + 1e-6)


def on_device(anomalies, grad_in, alpha, land_sea, length_rates, step_counts):
    nmem, levels, nx, ny = anomalies.shape
    ns, nm = lax.axis_size("slab"), lax.axis_size("mem")
    nall = ns * nm
    members_all = nmem * nm
    count_all = members_all * levels * nx * ns * ny
    f32 = jnp.float32
    vm = pl.BlockSpec(memory_space=pltpu.VMEM)
    dma = pltpu.SemaphoreType.DMA
    body = functools.partial(kernel, ns, nm, count_all, members_all)
    projected, stats = pl.pallas_call(
        body,
        out_shape=(
            jax.ShapeDtypeStruct(alpha.shape, f32),
            jax.ShapeDtypeStruct((2, 8, ny), f32),
        ),
        in_specs=[pl.BlockSpec(memory_space=pltpu.SMEM), vm, vm, vm, vm,
                  pl.BlockSpec(memory_space=pl.ANY)],
        out_specs=(pl.BlockSpec(memory_space=pl.ANY), vm),
        scratch_shapes=[
            pltpu.VMEM((levels, nx * nmem, ny), f32),
            pltpu.VMEM((levels, nx * nmem, ny), f32),
            pltpu.VMEM((nx * nmem, ny), f32),
            pltpu.VMEM((2, 2, levels, W * nmem, ny), f32),
            pltpu.VMEM((2, levels, W, ny), jnp.int32),
            pltpu.VMEM((2, 2, W, ny), f32),
            pltpu.VMEM((nx + 2 * W + 16, ny), f32),
            pltpu.VMEM((2, 2, levels, nx + 2 * W, ny), f32),
            pltpu.VMEM(alpha.shape, f32),
            pltpu.VMEM(alpha.shape, f32),
            pltpu.VMEM((levels, nx, ny), f32),
            pltpu.VMEM((max(nm - 1, 1), levels, nx, ny), f32),
            pltpu.VMEM((8, ny), f32),
            pltpu.VMEM((nall, 8, ny), f32),
            dma((2, 2, levels)), dma((2, 2, levels)),
            dma((2, 2)), dma((2, 2)),
            dma((max(nm - 1, 1), levels)), dma((max(nm - 1, 1), levels)),
            dma((nall,)), dma((nall,)),
            dma, dma((levels,)),
        ],
        compiler_params=pltpu.CompilerParams(
            collective_id=0, has_side_effects=True, vmem_limit_bytes=48 * 2**20
        ),
    )(step_counts, anomalies, grad_in, land_sea, length_rates, alpha)
    return (projected * stats[1, 0, 0], stats[0, 0, 0])


def solution(mesh):
    in_specs = (
        P("mem", None, "slab", None),
        P(None, "slab", None),
        P("mem", None, "slab", None),
        P(None, "slab", None),
        P(None, "slab", None),
        P(),
    )
    out_specs = (P("mem", None, "slab", None), P())
    return jax.shard_map(
        on_device, mesh=mesh, in_specs=in_specs, out_specs=out_specs, check_vma=False
    )
```

```python
import functools

import jax
import jax.numpy as jnp
from jax import lax
from jax.experimental import pallas as pl
from jax.experimental.pallas import tpu as pltpu
from jax.sharding import PartitionSpec as P

NSTEP = 8
SURE = 6
W = NSTEP
GROUP = 3
MESH = pl.DeviceIdType.MESH


def kernel(
    ns, nm, count_all, members_all,
    cnt_any, anom_any, gin_any, land_any, rate_any, alpha_any, proj_any, stats,
    cnt, anom, gin, land, rate, bk, ba, tri, ratio, u0, u1, u2, hal, ohal, rhal, oc, coef, alpha, g, sums, mean_all, tsend, trecv,
    hsend, hrecv, csend, crecv, msend, mrecv_sem, tsend_sem, trecv_sem, loc_sem,
    out_sem,
):
    nmem, levels, nx, ny = anom.shape
    s = lax.axis_index("slab")
    q = lax.axis_index("mem")
    left = (lax.rem(s + ns - 1, ns), q)
    right = (lax.rem(s + 1, ns), q)

    def along(d):
        return (lax.rem(s + d, ns), q)

    barrier = pltpu.get_barrier_semaphore()

    for d in range(1, ns):
        pl.semaphore_signal(barrier, inc=1, device_id=along(d), device_id_type=MESH)
    for d in range(1, nm):
        pl.semaphore_signal(barrier, inc=1, device_id=(s, lax.rem(q + d, nm)),
                            device_id_type=MESH)

    loads = [
        pltpu.make_async_copy(src, dst, loc_sem.at[i])
        for i, (src, dst) in enumerate((
            (land_any, land), (rate_any, rate), (gin_any, gin), (anom_any, anom),
            (cnt_any, cnt), (alpha_any, alpha)))
    ]
    for c in loads:
        c.start()
    loads[0].wait()
    loads[1].wait()
    pl.semaphore_wait(barrier, ns + nm - 2)

    def rdma(src, dst, ss, rs, dev):
        return pltpu.make_async_remote_copy(
            src_ref=src, dst_ref=dst, send_sem=ss, recv_sem=rs, device_id=dev,
            device_id_type=MESH,
        )

    def coef_copies():
        res = []
        for side, lo, dev in ((1, 0, left), (0, nx - W, right)):
            res.append(rdma(land.at[:, pl.ds(lo, W), :], ohal.at[side],
                            csend.at[0, side], crecv.at[0, side], dev))
            res.append(rdma(rate.at[:, pl.ds(lo, W), :], rhal.at[side],
                            csend.at[1, side], crecv.at[1, side], dev))
        return res

    def halo_copies(u, p, l):
        rows = W * nmem
        return [
            rdma(u.at[l, pl.ds(lo, rows), :], hal.at[p, side, l],
                 hsend.at[p, side, l], hrecv.at[p, side, l], dev)
            for side, lo, dev in ((1, 0, left), (0, nx * nmem - rows, right))
        ]

    def mean_copies(l):
        return [
            rdma(sums.at[0, l], sums.at[k, l], msend.at[k - 1, l],
                 mrecv_sem.at[k - 1, l], (s, lax.rem(q + k, nm)))
            for k in range(1, nm)
        ]

    def out_copy(l):
        return pltpu.make_async_copy(g.at[:, l], proj_any.at[:, l], out_sem.at[l])

    for c in coef_copies():
        c.start()
    loads[2].wait()
    loads[3].wait()

    @pl.loop(0, levels)
    def _(l):
        for h in range(nx // 16):
            facs = []
            for t in (2 * h, 2 * h + 1):
                sl = pl.ds(8 * t, 8)
                facs.append(gin[l, sl, :] * (rate[1, sl, :] * land[l, sl, :].astype(jnp.float32)))
            for m in range(nmem):
                a = anom[m, l, pl.ds(16 * h, 16), :].astype(jnp.float32)
                for j in range(2):
                    u0[l, pl.ds((16 * h + 8 * j) * nmem + m, 8, stride=nmem), :] = (
                        a[8 * j:8 * j + 8] * facs[j]
                    )
        for c in halo_copies(u0, 0, l):
            c.start()

    for c in coef_copies():
        c.wait()
    loads[4].wait()

    lane = lax.broadcasted_iota(jnp.int32, (8, ny), 1)
    not_first = lane > 0
    not_last = lane < ny - 1

    def sides(v):
        return (jnp.where(not_first, pltpu.roll(v, 1, 1), 0.0)
                + jnp.where(not_last, pltpu.roll(v, ny - 1, 1), 0.0))

    ext = nx + 2 * W
    zero = jnp.zeros((8, ny), jnp.float32)
    oc[pl.ds(0, 8), :] = zero
    oc[pl.ds(8 + ext, 8), :] = zero

    def rates_at(p, t):
        if t == 0:
            return rhal[0, p]
        if t == ext // 8 - 1:
            return rhal[1, p]
        return rate[p, pl.ds(8 * t - W, 8), :]

    ratio[...] = rate[0] / rate[1]

    def make_coefs(l):
        oc[pl.ds(8, 8), :] = ohal[0, l].astype(jnp.float32)
        for t in range(nx // 8):
            oc[pl.ds(8 + W + 8 * t, 8), :] = land[l, pl.ds(8 * t, 8), :].astype(jnp.float32)
        oc[pl.ds(8 + W + nx, 8), :] = ohal[1, l].astype(jnp.float32)
        for t in range(ext // 8):
            o = oc[pl.ds(8 + 8 * t, 8), :]
            around = oc[pl.ds(7 + 8 * t, 8), :] + oc[pl.ds(9 + 8 * t, 8), :] + sides(o)
            for p in (1, 0):
                k = o * rates_at(p, t)
                coef[p, 0, l, pl.ds(8 * t, 8), :] = k
                coef[p, 1, l, pl.ds(8 * t, 8), :] = 1.0 - k * around

    def wide(row):
        return jnp.broadcast_to(row, (nmem, ny))

    i = lax.broadcasted_iota(jnp.int32, (ny, ny), 0)
    j = lax.broadcasted_iota(jnp.int32, (ny, ny), 1)
    near = jnp.where(jnp.abs(i - j) == 1, 1.0, 0.0).astype(jnp.bfloat16)
    tri[pl.ds(0, ny), :] = near
    tri[pl.ds(ny, ny), :] = near

    def run(order, p, ls, src, put):
        masks, fields = [], []
        for n, l in enumerate(ls):
            steps = jnp.full((nmem, ny), cnt[p, l], jnp.int32)
            masks.append({t: steps >= t for t in range(SURE + 1, NSTEP + 1)})
            for x in range(1, ext - 1):
                bk[n, pl.ds(x * nmem, nmem), :] = wide(coef[p, 0, l, pl.ds(x, 1), :])
                ba[n, pl.ds(x * nmem, nmem), :] = wide(coef[p, 1, l, pl.ds(x, 1), :])
            fields.append(jnp.concatenate(
                [hal[order, 0, l], src[l], hal[order, 1, l]], axis=0))
        for t in range(1, NSTEP + 1):
            mids = [u[nmem:-nmem] for u in fields]
            rows = mids[0].shape[0]
            mid = jnp.concatenate(mids, axis=0)
            high = mid.astype(jnp.bfloat16)
            low = (mid - high.astype(jnp.float32)).astype(jnp.bfloat16)
            both = jnp.dot(jnp.concatenate([high, low], axis=1), tri[...],
                           preferred_element_type=jnp.float32)
            for n, u in enumerate(fields):
                at = pl.ds(t * nmem, rows)
                side = both[n * rows:(n + 1) * rows]
                new = ba[n, at, :] * mids[n] + bk[n, at, :] * (
                    (u[:-2 * nmem] + u[2 * nmem:]) + side)
                if t > SURE:
                    mask = masks[n][t]
                    new = jnp.concatenate(
                        [jnp.where(mask, new[x:x + nmem], mids[n][x:x + nmem])
                         for x in range(0, rows, nmem)], axis=0)
                fields[n] = new
        for n, l in enumerate(ls):
            for x in range(nx):
                put(n, l, x, fields[n][x * nmem:(x + 1) * nmem])

    @pl.loop(0, levels // GROUP)
    def _(b):
        ls = [b * GROUP + n for n in range(GROUP)]
        for l in ls:
            make_coefs(l)
            for c in halo_copies(u0, 0, l):
                c.wait_recv()

        def put(n, l, x, v):
            u1[l, pl.ds(x * nmem, nmem), :] = v * wide(ratio[pl.ds(x, 1), :])

        run(0, 1, ls, u0, put)
        for l in ls:
            for c in halo_copies(u1, 1, l):
                c.start()

    loads[5].wait()

    @pl.loop(0, levels // GROUP)
    def _(b):
        ls = [b * GROUP + n for n in range(GROUP)]
        for l in ls:
            for c in halo_copies(u1, 1, l):
                c.wait_recv()

        def put(n, l, x, v):
            u2[n, pl.ds(x * nmem, nmem), :] = v

        run(1, 0, ls, u1, put)
        for n, l in enumerate(ls):
            spread = zero
            for h in range(nx // 16):
                cs = []
                for t in (2 * h, 2 * h + 1):
                    sl = pl.ds(8 * t, 8)
                    cs.append((gin[l, sl, :], land[l, sl, :] > 0, 1.0 / rate[0, sl, :]))
                tot = [zero, zero]
                kept = [[], []]
                for m in range(nmem):
                    a = anom[m, l, pl.ds(16 * h, 16), :].astype(jnp.float32)
                    for j in range(2):
                        gi, wet, inv = cs[j]
                        x = 16 * h + 8 * j
                        u = u2[n, pl.ds(x * nmem + m, 8, stride=nmem), :]
                        v = alpha[m, l, pl.ds(x, 8), :] + jnp.where(wet, u * inv, a[8 * j:8 * j + 8] * gi)
                        g[m, l, pl.ds(x, 8), :] = v
                        tot[j] = tot[j] + v
                        kept[j].append(v)
                for j in range(2):
                    sums[0, l, pl.ds(16 * h + 8 * j, 8), :] = tot[j]
                    here = tot[j] * (1.0 / nmem)
                    for v in kept[j]:
                        spread = spread + (v - here) * (v - here)
            sums[0, l, pl.ds(nx, 8), :] = spread
            for c in mean_copies(l):
                c.start()

    order = [lax.rem(q - i + nm, nm) for i in range(nm)]

    def square(l, acc):
        for c in mean_copies(l):
            c.wait_recv()
        end = pl.ds(nx, 8)
        for k in order:
            acc = acc + sums[k, l, end, :]
        for t in range(nx // 8):
            sl = pl.ds(8 * t, 8)
            parts = [sums[k, l, sl, :] for k in order]
            mean = parts[0]
            for v in parts[1:]:
                mean = mean + v
            mean = mean * (1.0 / members_all)
            mean_all[l, sl, :] = mean
            for v in parts:
                gap = v * (1.0 / nmem) - mean
                acc = acc + nmem * (gap * gap)
        return acc

    own = lax.fori_loop(0, levels, square, zero)
    tsend[...] = own

    def total_copy(d):
        return rdma(tsend, trecv.at[d], tsend_sem.at[d], trecv_sem.at[d], along(d))

    for d in range(1, ns):
        total_copy(d).start()

    @pl.loop(0, levels)
    def _(l):
        for t in range(nx // 8):
            sl = pl.ds(8 * t, 8)
            mean = mean_all[l, sl, :]
            for m in range(nmem):
                g[m, l, sl, :] = g[m, l, sl, :] - mean
        out_copy(l).start()

    @pl.loop(0, levels)
    def _(l):
        for p, u in ((0, u0), (1, u1)):
            for c in halo_copies(u, p, l):
                c.wait_send()
        for c in mean_copies(l):
            c.wait_send()

    trecv[0] = own
    for d in range(1, ns):
        total_copy(d).wait()

    whole = zero
    for i in range(ns):
        whole = whole + trecv[lax.rem(s - i + ns, ns)]
    total = jnp.full((8, ny), jnp.sum(whole), jnp.float32)
    stats[0] = jnp.sqrt(total)
    stats[1] = 1.0 / jnp.sqrt(total * (1.0 / count_all) + 1e-6)

    @pl.loop(0, levels)
    def _(l):
        out_copy(l).wait()


def on_device(anomalies, grad_in, alpha, land_sea, length_rates, step_counts):
    nmem, levels, nx, ny = anomalies.shape
    ns, nm = lax.axis_size("slab"), lax.axis_size("mem")
    members_all = nmem * nm
    count_all = members_all * levels * nx * ns * ny
    f32 = jnp.float32
    vm = pl.BlockSpec(memory_space=pltpu.VMEM)
    dma = pltpu.SemaphoreType.DMA
    body = functools.partial(kernel, ns, nm, count_all, members_all)
    projected, stats = pl.pallas_call(
        body,
        out_shape=(
            jax.ShapeDtypeStruct(alpha.shape, f32),
            jax.ShapeDtypeStruct((2, 8, ny), f32),
        ),
        in_specs=[pl.BlockSpec(memory_space=pl.ANY)] * 6,
        out_specs=(pl.BlockSpec(memory_space=pl.ANY), vm),
        scratch_shapes=[
            pltpu.SMEM(step_counts.shape, jnp.int32),
            pltpu.VMEM(anomalies.shape, anomalies.dtype),
            pltpu.VMEM(grad_in.shape, f32),
            pltpu.VMEM(land_sea.shape, jnp.int32),
            pltpu.VMEM(length_rates.shape, f32),
            pltpu.VMEM((GROUP, (nx + 2 * W) * nmem, ny), f32),
            pltpu.VMEM((GROUP, (nx + 2 * W) * nmem, ny), f32),
            pltpu.VMEM((2 * ny, ny), jnp.bfloat16),
            pltpu.VMEM((nx, ny), f32),
            pltpu.VMEM((levels, nx * nmem, ny), f32),
            pltpu.VMEM((levels, nx * nmem, ny), f32),
            pltpu.VMEM((GROUP, nx * nmem, ny), f32),
            pltpu.VMEM((2, 2, levels, W * nmem, ny), f32),
            pltpu.VMEM((2, levels, W, ny), jnp.int32),
            pltpu.VMEM((2, 2, W, ny), f32),
            pltpu.VMEM((nx + 2 * W + 16, ny), f32),
            pltpu.VMEM((2, 2, levels, nx + 2 * W, ny), f32),
            pltpu.VMEM(alpha.shape, f32),
            pltpu.VMEM(alpha.shape, f32),
            pltpu.VMEM((nm, levels, nx + 8, ny), f32),
            pltpu.VMEM((levels, nx, ny), f32),
            pltpu.VMEM((8, ny), f32),
            pltpu.VMEM((ns, 8, ny), f32),
            dma((2, 2, levels)), dma((2, 2, levels)),
            dma((2, 2)), dma((2, 2)),
            dma((max(nm - 1, 1), levels)), dma((max(nm - 1, 1), levels)),
            dma((ns,)), dma((ns,)),
            dma((6,)), dma((levels,)),
        ],
        compiler_params=pltpu.CompilerParams(
            collective_id=0, has_side_effects=True, vmem_limit_bytes=48 * 2**20
        ),
    )(step_counts, anomalies, grad_in, land_sea, length_rates, alpha)
    return (projected * stats[1, 0, 0], stats[0, 0, 0])


def solution(mesh):
    in_specs = (
        P("mem", None, "slab", None),
        P(None, "slab", None),
        P("mem", None, "slab", None),
        P(None, "slab", None),
        P(None, "slab", None),
        P(),
    )
    out_specs = (P("mem", None, "slab", None), P())
    return jax.shard_map(
        on_device, mesh=mesh, in_specs=in_specs, out_specs=out_specs, check_vma=False
    )
```

```python
import functools

import jax
import jax.numpy as jnp
from jax import lax
from jax.experimental import pallas as pl
from jax.experimental.pallas import tpu as pltpu
from jax.sharding import PartitionSpec as P

NSTEP = 8
SURE = 6
W = NSTEP
GROUP = 3
MESH = pl.DeviceIdType.MESH


def kernel(
    ns, nm, count_all, members_all,
    cnt_any, anom_any, gin_any, land_any, rate_any, alpha_any, proj_any, stats,
    cnt, anom, gin, land, rate, bk, ba, tri, ratio, u0, u1, u2, hal, ohal, rhal, oc, coef, alpha, g, sums, mean_all, tsend, trecv,
    hsend, hrecv, csend, crecv, msend, mrecv_sem, tsend_sem, trecv_sem, loc_sem,
    out_sem,
):
    nmem, levels, nx, ny = anom.shape
    s = lax.axis_index("slab")
    q = lax.axis_index("mem")
    left = (lax.rem(s + ns - 1, ns), q)
    right = (lax.rem(s + 1, ns), q)

    def along(d):
        return (lax.rem(s + d, ns), q)

    barrier = pltpu.get_barrier_semaphore()

    for d in range(1, ns):
        pl.semaphore_signal(barrier, inc=1, device_id=along(d), device_id_type=MESH)
    for d in range(1, nm):
        pl.semaphore_signal(barrier, inc=1, device_id=(s, lax.rem(q + d, nm)),
                            device_id_type=MESH)

    loads = [
        pltpu.make_async_copy(src, dst, loc_sem.at[i])
        for i, (src, dst) in enumerate((
            (land_any, land), (rate_any, rate), (gin_any, gin), (anom_any, anom),
            (cnt_any, cnt), (alpha_any, alpha)))
    ]
    for c in loads:
        c.start()
    for c in loads[:4]:
        c.wait()

    def rdma(src, dst, ss, rs, dev):
        return pltpu.make_async_remote_copy(
            src_ref=src, dst_ref=dst, send_sem=ss, recv_sem=rs, device_id=dev,
            device_id_type=MESH,
        )

    def coef_copies():
        res = []
        for side, lo, dev in ((1, 0, left), (0, nx - W, right)):
            res.append(rdma(land.at[:, pl.ds(lo, W), :], ohal.at[side],
                            csend.at[0, side], crecv.at[0, side], dev))
            res.append(rdma(rate.at[:, pl.ds(lo, W), :], rhal.at[side],
                            csend.at[1, side], crecv.at[1, side], dev))
        return res

    def halo_copies(u, p, l):
        rows = W * nmem
        return [
            rdma(u.at[l, pl.ds(lo, rows), :], hal.at[p, side, l],
                 hsend.at[p, side, l], hrecv.at[p, side, l], dev)
            for side, lo, dev in ((1, 0, left), (0, nx * nmem - rows, right))
        ]

    def mean_copies(l):
        return [
            rdma(sums.at[0, l], sums.at[k, l], msend.at[k - 1, l],
                 mrecv_sem.at[k - 1, l], (s, lax.rem(q + k, nm)))
            for k in range(1, nm)
        ]

    def out_copy(l):
        return pltpu.make_async_copy(g.at[:, l], proj_any.at[:, l], out_sem.at[l])


    @pl.loop(0, levels)
    def _(l):
        for h in range(nx // 16):
            facs = []
            for t in (2 * h, 2 * h + 1):
                sl = pl.ds(8 * t, 8)
                facs.append(gin[l, sl, :] * (rate[1, sl, :] * land[l, sl, :].astype(jnp.float32)))
            for m in range(nmem):
                a = anom[m, l, pl.ds(16 * h, 16), :].astype(jnp.float32)
                for j in range(2):
                    u0[l, pl.ds((16 * h + 8 * j) * nmem + m, 8, stride=nmem), :] = (
                        a[8 * j:8 * j + 8] * facs[j]
                    )

    pl.semaphore_wait(barrier, ns + nm - 2)
    for c in coef_copies():
        c.start()

    @pl.loop(0, levels)
    def _(l):
        for c in halo_copies(u0, 0, l):
            c.start()

    for c in coef_copies():
        c.wait()
    loads[4].wait()

    lane = lax.broadcasted_iota(jnp.int32, (8, ny), 1)
    not_first = lane > 0
    not_last = lane < ny - 1

    def sides(v):
        return (jnp.where(not_first, pltpu.roll(v, 1, 1), 0.0)
                + jnp.where(not_last, pltpu.roll(v, ny - 1, 1), 0.0))

    ext = nx + 2 * W
    zero = jnp.zeros((8, ny), jnp.float32)
    oc[pl.ds(0, 8), :] = zero
    oc[pl.ds(8 + ext, 8), :] = zero

    def rates_at(p, t):
        if t == 0:
            return rhal[0, p]
        if t == ext // 8 - 1:
            return rhal[1, p]
        return rate[p, pl.ds(8 * t - W, 8), :]

    ratio[...] = rate[0] / rate[1]

    def make_coefs(l):
        oc[pl.ds(8, 8), :] = ohal[0, l].astype(jnp.float32)
        for t in range(nx // 8):
            oc[pl.ds(8 + W + 8 * t, 8), :] = land[l, pl.ds(8 * t, 8), :].astype(jnp.float32)
        oc[pl.ds(8 + W + nx, 8), :] = ohal[1, l].astype(jnp.float32)
        for t in range(ext // 8):
            o = oc[pl.ds(8 + 8 * t, 8), :]
            around = oc[pl.ds(7 + 8 * t, 8), :] + oc[pl.ds(9 + 8 * t, 8), :] + sides(o)
            for p in (1, 0):
                k = o * rates_at(p, t)
                coef[p, 0, l, pl.ds(8 * t, 8), :] = k
                coef[p, 1, l, pl.ds(8 * t, 8), :] = 1.0 - k * around

    def wide(row):
        return jnp.broadcast_to(row, (nmem, ny))

    i = lax.broadcasted_iota(jnp.int32, (ny, ny), 0)
    j = lax.broadcasted_iota(jnp.int32, (ny, ny), 1)
    near = jnp.where(jnp.abs(i - j) == 1, 1.0, 0.0).astype(jnp.bfloat16)
    tri[pl.ds(0, ny), :] = near
    tri[pl.ds(ny, ny), :] = near

    def run(order, p, ls, src, put):
        masks, fields = [], []
        for n, l in enumerate(ls):
            steps = jnp.full((nmem, ny), cnt[p, l], jnp.int32)
            masks.append({t: steps >= t for t in range(SURE + 1, NSTEP + 1)})
            for x in range(1, ext - 1):
                bk[n, pl.ds(x * nmem, nmem), :] = wide(coef[p, 0, l, pl.ds(x, 1), :])
                ba[n, pl.ds(x * nmem, nmem), :] = wide(coef[p, 1, l, pl.ds(x, 1), :])
            fields.append(jnp.concatenate(
                [hal[order, 0, l], src[l], hal[order, 1, l]], axis=0))
        for t in range(1, NSTEP + 1):
            mids = [u[nmem:-nmem] for u in fields]
            rows = mids[0].shape[0]
            mid = jnp.concatenate(mids, axis=0)
            high = mid.astype(jnp.bfloat16)
            low = (mid - high.astype(jnp.float32)).astype(jnp.bfloat16)
            both = jnp.dot(jnp.concatenate([high, low], axis=1), tri[...],
                           preferred_element_type=jnp.float32)
            for n, u in enumerate(fields):
                at = pl.ds(t * nmem, rows)
                side = both[n * rows:(n + 1) * rows]
                new = ba[n, at, :] * mids[n] + bk[n, at, :] * (
                    (u[:-2 * nmem] + u[2 * nmem:]) + side)
                if t > SURE:
                    mask = masks[n][t]
                    new = jnp.concatenate(
                        [jnp.where(mask, new[x:x + nmem], mids[n][x:x + nmem])
                         for x in range(0, rows, nmem)], axis=0)
                fields[n] = new
        for n, l in enumerate(ls):
            for x in range(nx):
                put(n, l, x, fields[n][x * nmem:(x + 1) * nmem])

    @pl.loop(0, levels // GROUP)
    def _(b):
        ls = [b * GROUP + n for n in range(GROUP)]
        for l in ls:
            make_coefs(l)
            for c in halo_copies(u0, 0, l):
                c.wait_recv()

        def put(n, l, x, v):
            u1[l, pl.ds(x * nmem, nmem), :] = v * wide(ratio[pl.ds(x, 1), :])

        run(0, 1, ls, u0, put)
        for l in ls:
            for c in halo_copies(u1, 1, l):
                c.start()

    loads[5].wait()

    @pl.loop(0, levels // GROUP)
    def _(b):
        ls = [b * GROUP + n for n in range(GROUP)]
        for l in ls:
            for c in halo_copies(u1, 1, l):
                c.wait_recv()

        def put(n, l, x, v):
            u2[n, pl.ds(x * nmem, nmem), :] = v

        run(1, 0, ls, u1, put)
        for n, l in enumerate(ls):
            spread = zero
            for h in range(nx // 16):
                cs = []
                for t in (2 * h, 2 * h + 1):
                    sl = pl.ds(8 * t, 8)
                    cs.append((gin[l, sl, :], land[l, sl, :] > 0, 1.0 / rate[0, sl, :]))
                tot = [zero, zero]
                kept = [[], []]
                for m in range(nmem):
                    a = anom[m, l, pl.ds(16 * h, 16), :].astype(jnp.float32)
                    for j in range(2):
                        gi, wet, inv = cs[j]
                        x = 16 * h + 8 * j
                        u = u2[n, pl.ds(x * nmem + m, 8, stride=nmem), :]
                        v = alpha[m, l, pl.ds(x, 8), :] + jnp.where(wet, u * inv, a[8 * j:8 * j + 8] * gi)
                        g[m, l, pl.ds(x, 8), :] = v
                        tot[j] = tot[j] + v
                        kept[j].append(v)
                for j in range(2):
                    sums[0, l, pl.ds(16 * h + 8 * j, 8), :] = tot[j]
                    here = tot[j] * (1.0 / nmem)
                    for v in kept[j]:
                        spread = spread + (v - here) * (v - here)
            sums[0, l, pl.ds(nx, 8), :] = spread
            for c in mean_copies(l):
                c.start()

    order = [lax.rem(q - i + nm, nm) for i in range(nm)]

    def square(l, acc):
        for c in mean_copies(l):
            c.wait_recv()
        end = pl.ds(nx, 8)
        for k in order:
            acc = acc + sums[k, l, end, :]
        for t in range(nx // 8):
            sl = pl.ds(8 * t, 8)
            parts = [sums[k, l, sl, :] for k in order]
            mean = parts[0]
            for v in parts[1:]:
                mean = mean + v
            mean = mean * (1.0 / members_all)
            mean_all[l, sl, :] = mean
            for v in parts:
                gap = v * (1.0 / nmem) - mean
                acc = acc + nmem * (gap * gap)
        return acc

    own = lax.fori_loop(0, levels, square, zero)
    tsend[...] = own

    def total_copy(d):
        return rdma(tsend, trecv.at[d], tsend_sem.at[d], trecv_sem.at[d], along(d))

    for d in range(1, ns):
        total_copy(d).start()

    @pl.loop(0, levels)
    def _(l):
        for t in range(nx // 8):
            sl = pl.ds(8 * t, 8)
            mean = mean_all[l, sl, :]
            for m in range(nmem):
                g[m, l, sl, :] = g[m, l, sl, :] - mean
        out_copy(l).start()

    @pl.loop(0, levels)
    def _(l):
        for p, u in ((0, u0), (1, u1)):
            for c in halo_copies(u, p, l):
                c.wait_send()
        for c in mean_copies(l):
            c.wait_send()

    trecv[0] = own
    for d in range(1, ns):
        total_copy(d).wait()

    whole = zero
    for i in range(ns):
        whole = whole + trecv[lax.rem(s - i + ns, ns)]
    total = jnp.full((8, ny), jnp.sum(whole), jnp.float32)
    stats[0] = jnp.sqrt(total)
    stats[1] = 1.0 / jnp.sqrt(total * (1.0 / count_all) + 1e-6)

    @pl.loop(0, levels)
    def _(l):
        out_copy(l).wait()


def on_device(anomalies, grad_in, alpha, land_sea, length_rates, step_counts):
    nmem, levels, nx, ny = anomalies.shape
    ns, nm = lax.axis_size("slab"), lax.axis_size("mem")
    members_all = nmem * nm
    count_all = members_all * levels * nx * ns * ny
    f32 = jnp.float32
    vm = pl.BlockSpec(memory_space=pltpu.VMEM)
    dma = pltpu.SemaphoreType.DMA
    body = functools.partial(kernel, ns, nm, count_all, members_all)
    projected, stats = pl.pallas_call(
        body,
        out_shape=(
            jax.ShapeDtypeStruct(alpha.shape, f32),
            jax.ShapeDtypeStruct((2, 8, ny), f32),
        ),
        in_specs=[pl.BlockSpec(memory_space=pl.ANY)] * 6,
        out_specs=(pl.BlockSpec(memory_space=pl.ANY), vm),
        scratch_shapes=[
            pltpu.SMEM(step_counts.shape, jnp.int32),
            pltpu.VMEM(anomalies.shape, anomalies.dtype),
            pltpu.VMEM(grad_in.shape, f32),
            pltpu.VMEM(land_sea.shape, jnp.int32),
            pltpu.VMEM(length_rates.shape, f32),
            pltpu.VMEM((GROUP, (nx + 2 * W) * nmem, ny), f32),
            pltpu.VMEM((GROUP, (nx + 2 * W) * nmem, ny), f32),
            pltpu.VMEM((2 * ny, ny), jnp.bfloat16),
            pltpu.VMEM((nx, ny), f32),
            pltpu.VMEM((levels, nx * nmem, ny), f32),
            pltpu.VMEM((levels, nx * nmem, ny), f32),
            pltpu.VMEM((GROUP, nx * nmem, ny), f32),
            pltpu.VMEM((2, 2, levels, W * nmem, ny), f32),
            pltpu.VMEM((2, levels, W, ny), jnp.int32),
            pltpu.VMEM((2, 2, W, ny), f32),
            pltpu.VMEM((nx + 2 * W + 16, ny), f32),
            pltpu.VMEM((2, 2, levels, nx + 2 * W, ny), f32),
            pltpu.VMEM(alpha.shape, f32),
            pltpu.VMEM(alpha.shape, f32),
            pltpu.VMEM((nm, levels, nx + 8, ny), f32),
            pltpu.VMEM((levels, nx, ny), f32),
            pltpu.VMEM((8, ny), f32),
            pltpu.VMEM((ns, 8, ny), f32),
            dma((2, 2, levels)), dma((2, 2, levels)),
            dma((2, 2)), dma((2, 2)),
            dma((max(nm - 1, 1), levels)), dma((max(nm - 1, 1), levels)),
            dma((ns,)), dma((ns,)),
            dma((6,)), dma((levels,)),
        ],
        compiler_params=pltpu.CompilerParams(
            collective_id=0, has_side_effects=True, vmem_limit_bytes=48 * 2**20
        ),
    )(step_counts, anomalies, grad_in, land_sea, length_rates, alpha)
    return (projected * stats[1, 0, 0], stats[0, 0, 0])


def solution(mesh):
    in_specs = (
        P("mem", None, "slab", None),
        P(None, "slab", None),
        P("mem", None, "slab", None),
        P(None, "slab", None),
        P(None, "slab", None),
        P(),
    )
    out_specs = (P("mem", None, "slab", None), P())
    return jax.shard_map(
        on_device, mesh=mesh, in_specs=in_specs, out_specs=out_specs, check_vma=False
    )
```

```python
import functools

import jax
import jax.numpy as jnp
from jax import lax
from jax.experimental import pallas as pl
from jax.experimental.pallas import tpu as pltpu
from jax.sharding import PartitionSpec as P

NSTEP = 8
SURE = 6
W = NSTEP
GROUP = 4
MESH = pl.DeviceIdType.MESH


def kernel(
    ns, nm, count_all, members_all,
    cnt_any, anom_any, gin_any, land_any, rate_any, alpha_any, proj_any, stats,
    cnt, anom, gin, land, rate, bk, ba, tri, ratio, u0, u1, u2, hal, ohal, rhal, oc, coef, alpha, g, sums, mean_all, tsend, trecv,
    hsend, hrecv, csend, crecv, msend, mrecv_sem, tsend_sem, trecv_sem, loc_sem,
    out_sem,
):
    nmem, levels, nx, ny = anom.shape
    s = lax.axis_index("slab")
    q = lax.axis_index("mem")
    left = (lax.rem(s + ns - 1, ns), q)
    right = (lax.rem(s + 1, ns), q)

    def along(d):
        return (lax.rem(s + d, ns), q)

    barrier = pltpu.get_barrier_semaphore()

    for d in range(1, ns):
        pl.semaphore_signal(barrier, inc=1, device_id=along(d), device_id_type=MESH)
    for d in range(1, nm):
        pl.semaphore_signal(barrier, inc=1, device_id=(s, lax.rem(q + d, nm)),
                            device_id_type=MESH)

    loads = [
        pltpu.make_async_copy(src, dst, loc_sem.at[i])
        for i, (src, dst) in enumerate((
            (land_any, land), (rate_any, rate), (gin_any, gin), (anom_any, anom),
            (cnt_any, cnt), (alpha_any, alpha)))
    ]
    for c in loads:
        c.start()
    for c in loads[:4]:
        c.wait()

    def rdma(src, dst, ss, rs, dev):
        return pltpu.make_async_remote_copy(
            src_ref=src, dst_ref=dst, send_sem=ss, recv_sem=rs, device_id=dev,
            device_id_type=MESH,
        )

    def coef_copies():
        res = []
        for side, lo, dev in ((1, 0, left), (0, nx - W, right)):
            res.append(rdma(land.at[:, pl.ds(lo, W), :], ohal.at[side],
                            csend.at[0, side], crecv.at[0, side], dev))
            res.append(rdma(rate.at[:, pl.ds(lo, W), :], rhal.at[side],
                            csend.at[1, side], crecv.at[1, side], dev))
        return res

    def halo_copies(u, p, l):
        rows = W * nmem
        return [
            rdma(u.at[l, pl.ds(lo, rows), :], hal.at[p, side, l],
                 hsend.at[p, side, l], hrecv.at[p, side, l], dev)
            for side, lo, dev in ((1, 0, left), (0, nx * nmem - rows, right))
        ]

    def mean_copies(l):
        return [
            rdma(sums.at[0, l], sums.at[k, l], msend.at[k - 1, l],
                 mrecv_sem.at[k - 1, l], (s, lax.rem(q + k, nm)))
            for k in range(1, nm)
        ]

    def out_copy(l):
        return pltpu.make_async_copy(g.at[:, l], proj_any.at[:, l], out_sem.at[l])


    @pl.loop(0, levels)
    def _(l):
        for h in range(nx // 16):
            facs = []
            for t in (2 * h, 2 * h + 1):
                sl = pl.ds(8 * t, 8)
                facs.append(gin[l, sl, :] * (rate[1, sl, :] * land[l, sl, :].astype(jnp.float32)))
            for m in range(nmem):
                a = anom[m, l, pl.ds(16 * h, 16), :].astype(jnp.float32)
                for j in range(2):
                    u0[l, pl.ds((16 * h + 8 * j) * nmem + m, 8, stride=nmem), :] = (
                        a[8 * j:8 * j + 8] * facs[j]
                    )

    pl.semaphore_wait(barrier, ns + nm - 2)
    for c in coef_copies():
        c.start()

    @pl.loop(0, levels)
    def _(l):
        for c in halo_copies(u0, 0, l):
            c.start()

    for c in coef_copies():
        c.wait()
    loads[4].wait()

    lane = lax.broadcasted_iota(jnp.int32, (8, ny), 1)
    not_first = lane > 0
    not_last = lane < ny - 1

    def sides(v):
        return (jnp.where(not_first, pltpu.roll(v, 1, 1), 0.0)
                + jnp.where(not_last, pltpu.roll(v, ny - 1, 1), 0.0))

    ext = nx + 2 * W
    zero = jnp.zeros((8, ny), jnp.float32)
    oc[pl.ds(0, 8), :] = zero
    oc[pl.ds(8 + ext, 8), :] = zero

    def rates_at(p, t):
        if t == 0:
            return rhal[0, p]
        if t == ext // 8 - 1:
            return rhal[1, p]
        return rate[p, pl.ds(8 * t - W, 8), :]

    ratio[...] = rate[0] / rate[1]

    def make_coefs(l):
        oc[pl.ds(8, 8), :] = ohal[0, l].astype(jnp.float32)
        for t in range(nx // 8):
            oc[pl.ds(8 + W + 8 * t, 8), :] = land[l, pl.ds(8 * t, 8), :].astype(jnp.float32)
        oc[pl.ds(8 + W + nx, 8), :] = ohal[1, l].astype(jnp.float32)
        for t in range(ext // 8):
            o = oc[pl.ds(8 + 8 * t, 8), :]
            around = oc[pl.ds(7 + 8 * t, 8), :] + oc[pl.ds(9 + 8 * t, 8), :] + sides(o)
            for p in (1, 0):
                k = o * rates_at(p, t)
                coef[p, 0, l, pl.ds(8 * t, 8), :] = k
                coef[p, 1, l, pl.ds(8 * t, 8), :] = 1.0 - k * around

    def wide(row):
        return jnp.broadcast_to(row, (nmem, ny))

    i = lax.broadcasted_iota(jnp.int32, (ny, ny), 0)
    j = lax.broadcasted_iota(jnp.int32, (ny, ny), 1)
    near = jnp.where(jnp.abs(i - j) == 1, 1.0, 0.0).astype(jnp.bfloat16)
    tri[pl.ds(0, ny), :] = near
    tri[pl.ds(ny, ny), :] = near

    def run(order, p, ls, src, put):
        masks, fields = [], []
        for n, l in enumerate(ls):
            steps = jnp.full((nmem, ny), cnt[p, l], jnp.int32)
            masks.append({t: steps >= t for t in range(SURE + 1, NSTEP + 1)})
            for x in range(1, ext - 1):
                bk[n, pl.ds(x * nmem, nmem), :] = wide(coef[p, 0, l, pl.ds(x, 1), :])
                ba[n, pl.ds(x * nmem, nmem), :] = wide(coef[p, 1, l, pl.ds(x, 1), :])
            fields.append(jnp.concatenate(
                [hal[order, 0, l], src[l], hal[order, 1, l]], axis=0))
        for t in range(1, NSTEP + 1):
            mids = [u[nmem:-nmem] for u in fields]
            rows = mids[0].shape[0]
            mid = jnp.concatenate(mids, axis=0)
            high = mid.astype(jnp.bfloat16)
            low = (mid - high.astype(jnp.float32)).astype(jnp.bfloat16)
            both = jnp.dot(jnp.concatenate([high, low], axis=1), tri[...],
                           preferred_element_type=jnp.float32)
            for n, u in enumerate(fields):
                at = pl.ds(t * nmem, rows)
                side = both[n * rows:(n + 1) * rows]
                new = ba[n, at, :] * mids[n] + bk[n, at, :] * (
                    (u[:-2 * nmem] + u[2 * nmem:]) + side)
                if t > SURE:
                    mask = masks[n][t]
                    new = jnp.concatenate(
                        [jnp.where(mask, new[x:x + nmem], mids[n][x:x + nmem])
                         for x in range(0, rows, nmem)], axis=0)
                fields[n] = new
        for n, l in enumerate(ls):
            for x in range(nx):
                put(n, l, x, fields[n][x * nmem:(x + 1) * nmem])

    @pl.loop(0, levels // GROUP)
    def _(b):
        ls = [b * GROUP + n for n in range(GROUP)]
        for l in ls:
            make_coefs(l)
            for c in halo_copies(u0, 0, l):
                c.wait_recv()

        def put(n, l, x, v):
            u1[l, pl.ds(x * nmem, nmem), :] = v * wide(ratio[pl.ds(x, 1), :])

        run(0, 1, ls, u0, put)
        for l in ls:
            for c in halo_copies(u1, 1, l):
                c.start()

    loads[5].wait()

    @pl.loop(0, levels // GROUP)
    def _(b):
        ls = [b * GROUP + n for n in range(GROUP)]
        for l in ls:
            for c in halo_copies(u1, 1, l):
                c.wait_recv()

        def put(n, l, x, v):
            u2[n, pl.ds(x * nmem, nmem), :] = v

        run(1, 0, ls, u1, put)
        for n, l in enumerate(ls):
            spread = zero
            for h in range(nx // 16):
                cs = []
                for t in (2 * h, 2 * h + 1):
                    sl = pl.ds(8 * t, 8)
                    cs.append((gin[l, sl, :], land[l, sl, :] > 0, 1.0 / rate[0, sl, :]))
                tot = [zero, zero]
                kept = [[], []]
                for m in range(nmem):
                    a = anom[m, l, pl.ds(16 * h, 16), :].astype(jnp.float32)
                    for j in range(2):
                        gi, wet, inv = cs[j]
                        x = 16 * h + 8 * j
                        u = u2[n, pl.ds(x * nmem + m, 8, stride=nmem), :]
                        v = alpha[m, l, pl.ds(x, 8), :] + jnp.where(wet, u * inv, a[8 * j:8 * j + 8] * gi)
                        g[m, l, pl.ds(x, 8), :] = v
                        tot[j] = tot[j] + v
                        kept[j].append(v)
                for j in range(2):
                    sums[0, l, pl.ds(16 * h + 8 * j, 8), :] = tot[j]
                    here = tot[j] * (1.0 / nmem)
                    for v in kept[j]:
                        spread = spread + (v - here) * (v - here)
            sums[0, l, pl.ds(nx, 8), :] = spread
            for c in mean_copies(l):
                c.start()

    order = [lax.rem(q - i + nm, nm) for i in range(nm)]

    def square(l, acc):
        for c in mean_copies(l):
            c.wait_recv()
        end = pl.ds(nx, 8)
        for k in order:
            acc = acc + sums[k, l, end, :]
        for t in range(nx // 8):
            sl = pl.ds(8 * t, 8)
            parts = [sums[k, l, sl, :] for k in order]
            mean = parts[0]
            for v in parts[1:]:
                mean = mean + v
            mean = mean * (1.0 / members_all)
            mean_all[l, sl, :] = mean
            for v in parts:
                gap = v * (1.0 / nmem) - mean
                acc = acc + nmem * (gap * gap)
        return acc

    own = lax.fori_loop(0, levels, square, zero)
    tsend[...] = own

    def total_copy(d):
        return rdma(tsend, trecv.at[d], tsend_sem.at[d], trecv_sem.at[d], along(d))

    for d in range(1, ns):
        total_copy(d).start()

    @pl.loop(0, levels)
    def _(l):
        for t in range(nx // 8):
            sl = pl.ds(8 * t, 8)
            mean = mean_all[l, sl, :]
            for m in range(nmem):
                g[m, l, sl, :] = g[m, l, sl, :] - mean
        out_copy(l).start()

    @pl.loop(0, levels)
    def _(l):
        for p, u in ((0, u0), (1, u1)):
            for c in halo_copies(u, p, l):
                c.wait_send()
        for c in mean_copies(l):
            c.wait_send()

    trecv[0] = own
    for d in range(1, ns):
        total_copy(d).wait()

    whole = zero
    for i in range(ns):
        whole = whole + trecv[lax.rem(s - i + ns, ns)]
    total = jnp.full((8, ny), jnp.sum(whole), jnp.float32)
    stats[0] = jnp.sqrt(total)
    stats[1] = 1.0 / jnp.sqrt(total * (1.0 / count_all) + 1e-6)

    @pl.loop(0, levels)
    def _(l):
        out_copy(l).wait()


def on_device(anomalies, grad_in, alpha, land_sea, length_rates, step_counts):
    nmem, levels, nx, ny = anomalies.shape
    ns, nm = lax.axis_size("slab"), lax.axis_size("mem")
    members_all = nmem * nm
    count_all = members_all * levels * nx * ns * ny
    f32 = jnp.float32
    vm = pl.BlockSpec(memory_space=pltpu.VMEM)
    dma = pltpu.SemaphoreType.DMA
    body = functools.partial(kernel, ns, nm, count_all, members_all)
    projected, stats = pl.pallas_call(
        body,
        out_shape=(
            jax.ShapeDtypeStruct(alpha.shape, f32),
            jax.ShapeDtypeStruct((2, 8, ny), f32),
        ),
        in_specs=[pl.BlockSpec(memory_space=pl.ANY)] * 6,
        out_specs=(pl.BlockSpec(memory_space=pl.ANY), vm),
        scratch_shapes=[
            pltpu.SMEM(step_counts.shape, jnp.int32),
            pltpu.VMEM(anomalies.shape, anomalies.dtype),
            pltpu.VMEM(grad_in.shape, f32),
            pltpu.VMEM(land_sea.shape, jnp.int32),
            pltpu.VMEM(length_rates.shape, f32),
            pltpu.VMEM((GROUP, (nx + 2 * W) * nmem, ny), f32),
            pltpu.VMEM((GROUP, (nx + 2 * W) * nmem, ny), f32),
            pltpu.VMEM((2 * ny, ny), jnp.bfloat16),
            pltpu.VMEM((nx, ny), f32),
            pltpu.VMEM((levels, nx * nmem, ny), f32),
            pltpu.VMEM((levels, nx * nmem, ny), f32),
            pltpu.VMEM((GROUP, nx * nmem, ny), f32),
            pltpu.VMEM((2, 2, levels, W * nmem, ny), f32),
            pltpu.VMEM((2, levels, W, ny), jnp.int32),
            pltpu.VMEM((2, 2, W, ny), f32),
            pltpu.VMEM((nx + 2 * W + 16, ny), f32),
            pltpu.VMEM((2, 2, levels, nx + 2 * W, ny), f32),
            pltpu.VMEM(alpha.shape, f32),
            pltpu.VMEM(alpha.shape, f32),
            pltpu.VMEM((nm, levels, nx + 8, ny), f32),
            pltpu.VMEM((levels, nx, ny), f32),
            pltpu.VMEM((8, ny), f32),
            pltpu.VMEM((ns, 8, ny), f32),
            dma((2, 2, levels)), dma((2, 2, levels)),
            dma((2, 2)), dma((2, 2)),
            dma((max(nm - 1, 1), levels)), dma((max(nm - 1, 1), levels)),
            dma((ns,)), dma((ns,)),
            dma((6,)), dma((levels,)),
        ],
        compiler_params=pltpu.CompilerParams(
            collective_id=0, has_side_effects=True, vmem_limit_bytes=48 * 2**20
        ),
    )(step_counts, anomalies, grad_in, land_sea, length_rates, alpha)
    return (projected * stats[1, 0, 0], stats[0, 0, 0])


def solution(mesh):
    in_specs = (
        P("mem", None, "slab", None),
        P(None, "slab", None),
        P("mem", None, "slab", None),
        P(None, "slab", None),
        P(None, "slab", None),
        P(),
    )
    out_specs = (P("mem", None, "slab", None), P())
    return jax.shard_map(
        on_device, mesh=mesh, in_specs=in_specs, out_specs=out_specs, check_vma=False
    )
```
